128 devices in a mesh: dp: 8 (over y_lo, x), tensor: 16 (over z, y_hi, core).
Axes of the slice: x: 4, y: 4 (y_hi: 2, y_lo: 2; y = y_hi * 2 + y_lo), z: 4, core: 2. Of those that a mesh axis runs over, the one named last changes fastest.
Arguments:
- images: bfloat16 [8, 1024, 1024], P('dp'), may hold values from -6 to 6
- w_qkv: bfloat16 [1, 1024, 3072], P(None, None, 'tensor'), may hold values from -0.1875 to 0.1875
- bias_query: float32 [1, 1024], P(None, 'tensor'), may hold values from -3 to 3
- bias_value: float32 [1, 1024], P(None, 'tensor'), may hold values from -3 to 3
- w_out: bfloat16 [1, 1024, 1024], P(None, 'tensor'), may hold values from -0.1875 to 0.1875
- bias_out: float32 [1, 1024], replicated, may hold values from -3 to 3
- w_up: bfloat16 [1, 1024, 4096], P(None, None, 'tensor'), may hold values from -0.1875 to 0.1875
- bias_up: float32 [1, 4096], P(None, 'tensor'), may hold values from -3 to 3
- w_down: bfloat16 [1, 4096, 1024], P(None, 'tensor'), may hold values from -0.09375 to 0.09375
- bias_down: float32 [1, 1024], replicated, may hold values from -3 to 3
- norm1_gain: float32 [1, 1024], replicated, may hold values from 0.5 to 1.5
- norm1_shift: float32 [1, 1024], replicated, may hold values from -3 to 3
- norm2_gain: float32 [1, 1024], replicated, may hold values from 0.5 to 1.5
- norm2_shift: float32 [1, 1024], replicated, may hold values from -3 to 3
- scale_attn: float32 [1, 1024], replicated, may hold values from 0.5 to 1.5
- scale_mlp: float32 [1, 1024], replicated, may hold values from 0.5 to 1.5
- cotangent: bfloat16 [8, 1024, 1024], P('dp'), may hold values from -6 to 6
Outputs:
- final: float32 [8, 1024, 1024], P('dp')
- grad_input: float32 [8, 1024, 1024], P('dp')
- grad_qkv: float32 [1, 1024, 3072], P(None, 'dp', 'tensor')
- grad_query_bias: float32 [1, 1024], P(None, 'tensor')
- grad_value_bias: float32 [1, 1024], P(None, 'tensor')
- grad_out: float32 [1, 1024, 1024], P(None, 'tensor', 'dp')
- grad_out_bias: float32 [1, 1024], replicated
- grad_up: float32 [1, 1024, 4096], P(None, 'dp', 'tensor')
- grad_up_bias: float32 [1, 4096], P(None, 'tensor')
- grad_down: float32 [1, 4096, 1024], P(None, 'tensor', 'dp')
- grad_down_bias: float32 [1, 1024], replicated
- grad_norm1_gain: float32 [1, 1024], replicated
- grad_norm1_shift: float32 [1, 1024], replicated
- grad_norm2_gain: float32 [1, 1024], replicated
- grad_norm2_shift: float32 [1, 1024], replicated
- grad_scale_attn: float32 [1, 1024], replicated
- grad_scale_mlp: float32 [1, 1024], replicated
The draws below stay inside these ranges and needn't reach their ends.
All inputs are finite; a program needn't handle non-finite values.
Results may differ from the reference program's by a relative error of at most 0.015.
The reference program's roundings to bfloat16 on the way count: a program that leaves them out, or rounds other values in their place, can miss the bound.
Values sent between devices are 32-bit elements; how exact they have to be, the bound alone decides.
No kernel may reach another device: no remote copies, remote signals or barrier semaphores. Data moves between devices by JAX's collectives and lax.ppermute only.
A program may use at most 128 MiB of HBM per device.

```python
import jax
import jax.numpy as jnp
from jax import lax

D = 1024
HEADS = 16
DH = 64
FF = 4096
SEQ = 1024
LAYERS = 1
IMAGES = 8


def levels(key, dims, cuts, smallest, largest):
    def one(axis_at, parts):
        steps = jax.random.uniform(jax.random.fold_in(jax.random.fold_in(key, 6), axis_at), (parts,), jnp.float32, smallest / len(cuts), largest / len(cuts))
        return jnp.repeat(jnp.exp(steps), dims[axis_at] // parts).reshape((-1,) + (1,) * (len(dims) - axis_at - 1))

    level = one(*cuts[0])
    for cut in cuts[1:]:
        level = level * one(*cut)
    return level


def normal_values(own_key, extent, scale, bound, shards=(), kind=jnp.bfloat16):
    level = levels(own_key, extent, shards, -0.22, 0.18) if shards else 1.0
    entries = jax.random.normal(own_key, extent, jnp.float32) * scale * level
    return jnp.minimum(jnp.maximum(entries, -bound), bound).astype(kind)


def setup_inputs(seed: int = 0) -> dict:
    seeds = jax.random.split(jax.random.key(seed), 18)
    return {
        "images": normal_values(seeds[0], (IMAGES, SEQ, D), 1.0, 6.0, ((0, 8),)),
        "w_qkv": normal_values(seeds[1], (LAYERS, D, 3 * D), D ** -0.5, 0.1875, ((2, 16),)),
        "bias_query": normal_values(seeds[2], (LAYERS, D), 0.5, 3.0, ((1, 16),), jnp.float32),
        "bias_value": normal_values(seeds[3], (LAYERS, D), 0.5, 3.0, ((1, 16),), jnp.float32),
        "w_out": normal_values(seeds[4], (LAYERS, D, D), D ** -0.5, 0.1875, ((1, 16),)),
        "bias_out": normal_values(seeds[5], (LAYERS, D), 0.5, 3.0, (), jnp.float32),
        "w_up": normal_values(seeds[6], (LAYERS, D, FF), D ** -0.5, 0.1875, ((2, 16),)),
        "bias_up": normal_values(seeds[7], (LAYERS, FF), 0.5, 3.0, ((1, 16),), jnp.float32),
        "w_down": normal_values(seeds[8], (LAYERS, FF, D), FF ** -0.5, 0.09375, ((1, 16),)),
        "bias_down": normal_values(seeds[9], (LAYERS, D), 0.5, 3.0, (), jnp.float32),
        "norm1_gain": jnp.clip(1.0 + 0.1 * jax.random.normal(seeds[10], (LAYERS, D), jnp.float32), 0.5, 1.5),
        "norm1_shift": normal_values(seeds[11], (LAYERS, D), 0.5, 3.0, (), jnp.float32),
        "norm2_gain": jnp.clip(1.0 + 0.1 * jax.random.normal(seeds[12], (LAYERS, D), jnp.float32), 0.5, 1.5),
        "norm2_shift": normal_values(seeds[13], (LAYERS, D), 0.5, 3.0, (), jnp.float32),
        "scale_attn": jnp.clip(jax.random.uniform(seeds[14], (LAYERS, D), jnp.float32, 0.5, 1.5), 0.5, 1.5),
        "scale_mlp": jnp.clip(jax.random.uniform(seeds[15], (LAYERS, D), jnp.float32, 0.5, 1.5), 0.5, 1.5),
        "cotangent": normal_values(seeds[16], (IMAGES, SEQ, D), 1.0, 6.0, ((0, 8),)),
    }


@jax.custom_vjp
def low(v):
    return lax.optimization_barrier(v.astype(jnp.bfloat16)).astype(jnp.float32)

@jax.custom_vjp
def low_back(v):
    return v

def low_keep(v):
    return (low(v), None)

def low_pass(kept, grad):
    return (grad,)

def back_keep(v):
    return (v, None)

def back_low(kept, grad):
    return (low(grad),)
low.defvjp(low_keep, low_pass)
low_back.defvjp(back_keep, back_low)
eps_norm = 1e-06
highest = lax.Precision.HIGHEST

def round_both(values):
    return low_back(low(values))

def norm_rows(values, gain, shift):
    centre = lax.optimization_barrier(jnp.mean(values, axis=-1, keepdims=True))
    shifted = values - centre
    spread = lax.optimization_barrier(jnp.mean(shifted * shifted, axis=-1, keepdims=True))
    return shifted * lax.rsqrt(spread + eps_norm) * gain + shift

def one_layer(params, inputs):
    normed = low(norm_rows(inputs, params['n1g'], params['n1b']))
    mixed = jnp.dot(normed, params['wqkv'], precision=highest).reshape(SEQ, HEADS, 3, DH)
    query = round_both(mixed[:, :, 0] + params['bq'].reshape(HEADS, DH))
    key_vec = round_both(mixed[:, :, 1])
    value = round_both(mixed[:, :, 2] + params['bv'].reshape(HEADS, DH))
    scores = low_back(jnp.einsum('qhd,khd->hqk', query, key_vec, precision=highest) * DH ** (-0.5))
    peak = lax.optimization_barrier(jnp.max(scores, axis=-1, keepdims=True))
    expo = jnp.exp(scores - peak)
    probs = low(expo / lax.optimization_barrier(jnp.sum(expo, axis=-1, keepdims=True)))
    context = round_both(jnp.einsum('hqk,khd->qhd', probs, value, precision=highest).reshape(SEQ, D))
    attended = low_back(jnp.dot(context, params['wo'], precision=highest) + params['bo'])
    middle = inputs + params['s1'] * attended
    normed_two = low(norm_rows(middle, params['n2g'], params['n2b']))
    before = low_back(jnp.dot(normed_two, params['wup'], precision=highest) + params['bup'])
    active = low(jax.nn.gelu(before, approximate=False))
    perceptron = low_back(jnp.dot(active, params['wdown'], precision=highest) + params['bdown'])
    return middle + params['s2'] * perceptron

def reference(images, w_qkv, bias_query, bias_value, w_out, bias_out, w_up, bias_up, w_down, bias_down, norm1_gain, norm1_shift, norm2_gain, norm2_shift, scale_attn, scale_mlp, cotangent):
    params = {'wqkv': w_qkv, 'bq': bias_query, 'bv': bias_value, 'wo': w_out, 'bo': bias_out, 'wup': w_up, 'bup': bias_up, 'wdown': w_down, 'bdown': bias_down, 'n1g': norm1_gain, 'n1b': norm1_shift, 'n2g': norm2_gain, 'n2b': norm2_shift, 's1': scale_attn, 's2': scale_mlp}
    params = jax.tree.map(lambda leaf: leaf.astype(jnp.float32), params)

    def forward(weights, inputs):
        current = inputs
        for layer_idx in range(LAYERS):
            current = one_layer(jax.tree.map(lambda leaf: leaf[layer_idx], weights), current)
        return current
    zeros = jax.tree.map(jnp.zeros_like, params)

    def image_step(running, couple):
        inputs, grad_seed = couple
        output, pullback = jax.vjp(forward, params, inputs)
        grad_params, grad_inputs = pullback(grad_seed)
        return (jax.tree.map(jnp.add, running, grad_params), (output, grad_inputs))
    summed, (outputs, grad_inputs) = lax.scan(image_step, zeros, (images.astype(jnp.float32), cotangent.astype(jnp.float32)))
    return (outputs, grad_inputs, summed['wqkv'], summed['bq'], summed['bv'], summed['wo'], summed['bo'], summed['wup'], summed['bup'], summed['wdown'], summed['bdown'], summed['n1g'], summed['n1b'], summed['n2g'], summed['n2b'], summed['s1'], summed['s2'])
```

```python
import jax
import jax.numpy as jnp
from jax import lax
from jax.experimental import pallas as pl
from jax.experimental.pallas import tpu as pltpu
from jax.sharding import Mesh, PartitionSpec as P

DH = 64
EPS = 1e-06
BF = jnp.bfloat16
F32 = jnp.float32
DATA = ("yl", "x")
TENSOR = ("z", "yh", "c")
FACTOR = DH ** (-0.5)
VMEM_BYTES = 48 * 1024 * 1024


def from_core(v):
    return lax.ppermute(v, "c", [(0, 1), (1, 0)])


def from_yh(v):
    return lax.ppermute(v, "yh", [(0, 1), (1, 0)])


def from_z(v, k):
    return lax.ppermute(v, "z", [((i + k) % 4, i) for i in range(4)])


def from_chip(v, k, j):
    pairs = [
        (((z + k) % 4) * 2 + (y ^ j), z * 2 + y) for z in range(4) for y in range(2)
    ]
    return lax.ppermute(v, ("z", "yh"), pairs)


def gather_half(s):
    h = s.shape[0] // 2
    y = from_yh(s)
    a1, a3 = from_z(s, 1), from_z(s, 3)
    b1, b3 = from_z(y, 1), from_z(y, 3)
    a2t, a2b = from_z(a1[:h], 1), from_z(a3[h:], 3)
    b2t, b2b = from_z(b1[:h], 1), from_z(b3[h:], 3)
    return [s, y, a1, b1, jnp.concatenate([a2t, a2b]), jnp.concatenate([b2t, b2b]), a3, b3]


def gather_rows(s):
    half = jnp.concatenate(gather_half(s))
    return jnp.concatenate([half, from_core(half)])


def scatter_rows(p):
    q = p[:512] + from_core(p[512:])
    blk = lambda k, j: q[k * 128 + j * 64 : k * 128 + j * 64 + 64]
    t = from_z(blk(2, 0), 3)
    r = from_z(blk(2, 1), 1)
    e1 = from_z(blk(1, 1), 3)
    e0 = from_z(blk(3, 0), 1)
    f0 = from_z(blk(1, 0) + t, 3)
    f1 = from_z(blk(3, 1) + r, 1)
    s1 = blk(0, 1) + e1 + f1
    s0 = blk(0, 0) + e0 + f0
    return s0 + from_yh(s1)


def heads_to_rows(h):
    m = jnp.concatenate([h[:512], from_core(h[512:])], axis=1)
    got = []
    for k in range(4):
        for j in range(2):
            at = (((-k) % 4) * 2 + j) * 64
            piece = m[at : at + 64]
            got.append(piece if k == j == 0 else from_chip(piece, k, j))
    return jnp.concatenate(got, axis=1)


def rows_to_heads(g):
    got = []
    for k in range(4):
        for j in range(2):
            at = (((-k) % 4) * 2 + j) * 128
            piece = g[:, at : at + 128]
            got.append(piece if k == j == 0 else from_chip(piece, k, j))
    m = jnp.concatenate(got, axis=0)
    return jnp.concatenate([m[:, :64], from_core(m[:, 64:])], axis=0)


def butterfly(v, axis, size):
    step = 1
    while step < size:
        v = v + lax.ppermute(v, axis, [(i, i ^ step) for i in range(size)])
        step *= 2
    return v


def normalize(values):
    centre = jnp.mean(values, axis=-1, keepdims=True)
    shifted = values - centre
    spread = jnp.mean(shifted * shifted, axis=-1, keepdims=True)
    inv_std = lax.rsqrt(spread + EPS)
    return shifted * inv_std, inv_std


def norm_back(grad_normed, x_hat, inv_std, gain):
    grad_hat = grad_normed * gain
    first = jnp.mean(grad_hat, axis=-1, keepdims=True)
    second = jnp.mean(grad_hat * x_hat, axis=-1, keepdims=True)
    return inv_std * (grad_hat - first - x_hat * second)


def mm(a, b):
    return jnp.dot(a, b, preferred_element_type=F32)


def mmt(a, b):
    return lax.dot_general(a, b, (((1,), (1,)), ((), ())), preferred_element_type=F32)


def tmm(a, b):
    return lax.dot_general(a, b, (((0,), (0,)), ((), ())), preferred_element_type=F32)


def rows(v):
    return jnp.sum(v, axis=0, keepdims=True)


def shape(dims, dtype=F32):
    return jax.ShapeDtypeStruct(dims, dtype)


def params():
    return pltpu.CompilerParams(vmem_limit_bytes=VMEM_BYTES)


def cost(gflop, mb):
    return pl.CostEstimate(
        flops=int(gflop * 1e9), bytes_accessed=int(mb * 1e6), transcendentals=0
    )


def attn_forward_kernel(starts, x, w, bq, bv, gain, shift, a, q, k, v, lse, ctx32, ctx_t, v_t):
    gain_v, shift_v = gain[...], shift[...]
    for n in range(8):
        lo, hi = starts[2 * n], starts[2 * n + 1]
        rows_n = jnp.concatenate(
            [x[pl.ds(pl.multiple_of(lo, 64), 64)], x[pl.ds(pl.multiple_of(hi, 64), 64)]]
        ).astype(F32)
        x_hat, _ = normalize(rows_n)
        a_n = (x_hat * gain_v + shift_v).astype(BF)
        here = pl.ds(n * 128, 128)
        a[here] = a_n
        mixed = mm(a_n, w[...])
        q[here] = (mixed[:, :64] + bq[...]).astype(BF)
        k[here] = mixed[:, 64:128].astype(BF)
        v_n = (mixed[:, 128:] + bv[...]).astype(BF)
        v[here] = v_n
        v_t[:, here] = v_n.astype(F32).T.astype(BF)
    for n in range(4):
        here = pl.ds(n * 256, 256)
        scores = mmt(k[...], q[here]) * FACTOR
        peak = jnp.max(scores, axis=0, keepdims=True)
        expo = jnp.exp(scores - peak)
        denom = jnp.sum(expo, axis=0, keepdims=True)
        probs = (expo / denom).astype(BF)
        lse[:, here] = peak + jnp.log(denom)
        ctx = mm(v_t[...], probs)
        ctx_t[:, here] = ctx.astype(BF)
        ctx32[here] = ctx.T


def attn_forward(starts, images, w, bq, bv, gain, shift):
    vm = pl.BlockSpec(memory_space=pltpu.VMEM)
    small = shape((1024, 64), BF)
    return pl.pallas_call(
        attn_forward_kernel,
        out_shape=(
            shape((1024, 1024), BF),
            small,
            small,
            small,
            shape((1, 1024)),
            shape((1024, 64)),
            shape((64, 1024), BF),
        ),
        in_specs=[pl.BlockSpec(memory_space=pltpu.SMEM)] + [vm] * 6,
        out_specs=[vm] * 7,
        scratch_shapes=[pltpu.VMEM((64, 1024), BF)],
        compiler_params=params(),
        cost_estimate=cost(5, 8),
        name="attn_forward",
    )(starts, images, w, bq, bv, gain, shift)


def grad_rows_kernel(starts, g, scale, gm):
    gm[...] = (g[...].astype(F32) * scale[...]).astype(BF)


def grad_rows(starts, cotangent, scale):
    return pl.pallas_call(
        grad_rows_kernel,
        out_shape=shape((1024, 1024), BF),
        grid_spec=pltpu.PrefetchScalarGridSpec(
            num_scalar_prefetch=1,
            grid=(16,),
            in_specs=[
                pl.BlockSpec((64, 1024), lambda n, s: (s[n] // 64, 0)),
                pl.BlockSpec((1, 1024), lambda n, s: (0, 0)),
            ],
            out_specs=pl.BlockSpec((64, 1024), lambda n, s: (n, 0)),
        ),
        compiler_params=params(),
        cost_estimate=cost(0.01, 8),
        name="grad_rows",
    )(starts, cotangent, scale)


def round_weights_kernel(mine, other, out):
    out[0:64] = mine[...].astype(BF)
    out[64:128] = other[...].astype(BF)


def round_weights(mine, other):
    part = pl.BlockSpec((64, 1024), lambda n: (n, 0))
    return pl.pallas_call(
        round_weights_kernel,
        out_shape=shape((1024, 1024), BF),
        grid=(8,),
        in_specs=[part, part],
        out_specs=pl.BlockSpec((128, 1024), lambda n: (n, 0)),
        compiler_params=params(),
        cost_estimate=cost(0.01, 8),
        name="round_weights",
    )(mine, other)


def middle_kernel(ctx, w, x, bias, scale, gain, shift, attn, hmid, b_hat, b_std, b):
    y = mm(ctx[...].astype(BF), w[...]) + bias[...]
    attn[...] = y
    h = x[...] + scale[...] * y
    hmid[...] = h
    hat, std = normalize(h)
    b_hat[...] = hat
    b_std[...] = std
    b[...] = hat * gain[...] + shift[...]


def middle(ctx, w, x, bias, scale, gain, shift):
    wide = shape((64, 1024))
    return pl.pallas_call(
        middle_kernel,
        out_shape=(wide, wide, wide, shape((64, 1)), wide),
        compiler_params=params(),
        cost_estimate=cost(0.2, 3),
        name="middle",
    )(ctx, w, x, bias, scale, gain, shift)


def mlp_kernel(b32, gm, w_up, w_down, bias, gb, b, act, gpre, total):
    b_n = b32[...].astype(BF)
    b[...] = b_n
    pre = mm(b_n, w_up[...]) + bias[...]
    cdf = 0.5 * (1.0 + lax.erf(pre * (0.5**0.5)))
    act[...] = (pre * cdf).astype(BF)
    slope = cdf + pre * (jnp.exp(-0.5 * pre * pre) * 0.3989422804014327)
    gact = mmt(gm[...], w_down[...])
    gpre_n = (gact * slope).astype(BF)
    gpre[...] = gpre_n
    gb[...] = mmt(gpre_n, w_up[...])

    @pl.when(pl.program_id(0) == 0)
    def _():
        total[...] = jnp.zeros_like(total)

    total[...] += rows(gpre_n.astype(F32))


def mlp(b32, gm, w_up, w_down, bias):
    rows_in = pl.BlockSpec((256, 1024), lambda n: (n, 0))
    rows_ff = pl.BlockSpec((256, 256), lambda n: (n, 0))
    whole = lambda *dims: pl.BlockSpec(dims, lambda n: (0, 0))
    return pl.pallas_call(
        mlp_kernel,
        out_shape=(
            shape((1024, 1024)),
            shape((1024, 1024), BF),
            shape((1024, 256), BF),
            shape((1024, 256), BF),
            shape((1, 256)),
        ),
        grid=(4,),
        in_specs=[rows_in, rows_in, whole(1024, 256), whole(256, 1024), whole(1, 256)],
        out_specs=[rows_in, rows_in, rows_ff, rows_ff, whole(1, 256)],
        compiler_params=params(),
        cost_estimate=cost(3, 14),
        name="mlp",
    )(b32, gm, w_up, w_down, bias)


def attn_backward_kernel(q, k, v, lse, gctx, mixed, k_t, gq_t, gk, gv):
    n = pl.program_id(0)

    @pl.when(n == 0)
    def _():
        gk[...] = jnp.zeros_like(gk)
        gv[...] = jnp.zeros_like(gv)
        k_t[...] = k[...].astype(F32).T.astype(BF)

    gctx_n = gctx[...].astype(BF)
    q_n = q[...]
    p = jnp.exp(mmt(k[...], q_n) * FACTOR - lse[...])
    gv[...] += mm(p.astype(BF), gctx_n)
    gp = mmt(v[...], gctx_n)
    gs = (p * (gp - jnp.sum(p * gp, axis=0, keepdims=True))).astype(BF)
    gk[...] += mm(gs, q_n)
    gq_t[:, pl.ds(pl.multiple_of(n * 256, 256), 256)] = mm(k_t[...], gs)

    @pl.when(n == 3)
    def _():
        mixed[...] = jnp.concatenate(
            [gq_t[...].T * FACTOR, gk[...] * FACTOR, gv[...]], axis=1
        ).astype(BF)


def attn_backward(q, k, v, lse, gctx):
    part = pl.BlockSpec((256, 64), lambda n: (n, 0))
    whole = lambda *dims: pl.BlockSpec(dims, lambda n: (0, 0))
    return pl.pallas_call(
        attn_backward_kernel,
        out_shape=shape((1024, 192), BF),
        grid=(4,),
        in_specs=[
            part,
            whole(1024, 64),
            whole(1024, 64),
            pl.BlockSpec((1, 256), lambda n: (0, n)),
            part,
        ],
        out_specs=whole(1024, 192),
        scratch_shapes=[
            pltpu.VMEM((64, 1024), BF),
            pltpu.VMEM((64, 1024), F32),
            pltpu.VMEM((1024, 64), F32),
            pltpu.VMEM((1024, 64), F32),
        ],
        compiler_params=params(),
        cost_estimate=cost(6, 2),
        name="attn_backward",
    )(q, k, v, lse, gctx)


def input_grad_kernel(starts, lo, hi, mixed, w, part, sums, cols):
    x_hat, _ = normalize(jnp.concatenate([lo[...], hi[...]]).astype(F32))
    y = mmt(mixed[...], w[...])
    part[...] = y

    @pl.when(pl.program_id(0) == 0)
    def _():
        sums[...] = jnp.zeros_like(sums)
        cols[...] = jnp.zeros_like(cols)

    sums[0:1] += rows(y * x_hat)
    sums[1:2] += rows(y)
    cols[...] += rows(mixed[...].astype(F32))


def input_grad(starts, images, mixed, w):
    return pl.pallas_call(
        input_grad_kernel,
        out_shape=(shape((1024, 1024)), shape((2, 1024)), shape((1, 192))),
        grid_spec=pltpu.PrefetchScalarGridSpec(
            num_scalar_prefetch=1,
            grid=(8,),
            in_specs=[
                pl.BlockSpec((64, 1024), lambda n, s: (s[2 * n] // 64, 0)),
                pl.BlockSpec((64, 1024), lambda n, s: (s[2 * n + 1] // 64, 0)),
                pl.BlockSpec((128, 192), lambda n, s: (n, 0)),
                pl.BlockSpec((1024, 192), lambda n, s: (0, 0)),
            ],
            out_specs=[
                pl.BlockSpec((128, 1024), lambda n, s: (n, 0)),
                pl.BlockSpec((2, 1024), lambda n, s: (0, 0)),
                pl.BlockSpec((1, 192), lambda n, s: (0, 0)),
            ],
        ),
        compiler_params=params(),
        cost_estimate=cost(1, 6),
        name="input_grad",
    )(starts, images, images, mixed, w)


def out_grad_kernel(ctx_t, ga, out):
    out[...] = mm(ctx_t[...], ga[...].astype(BF)).T


def out_grad(ctx_t, ga):
    return pl.pallas_call(
        out_grad_kernel,
        out_shape=shape((1024, 64)),
        compiler_params=params(),
        cost_estimate=cost(0.2, 5),
        name="out_grad",
    )(ctx_t, ga)


def on_device(
    images,
    w_qkv,
    bias_query,
    bias_value,
    w_out,
    bias_out,
    w_up,
    bias_up,
    w_down,
    bias_down,
    norm1_gain,
    norm1_shift,
    norm2_gain,
    norm2_shift,
    scale_attn,
    scale_mlp,
    cotangent,
):
    w_qkv, w_out, w_up, w_down = w_qkv[0], w_out[0], w_up[0], w_down[0]
    images, cotangent = images[0], cotangent[0]
    c, z, yh = lax.axis_index("c"), lax.axis_index("z"), lax.axis_index("yh")
    starts = jnp.stack(
        [
            (((c + i) % 2) * 8 + ((z + k) % 4) * 2 + ((yh + j) % 2)) * 64
            for i in range(2)
            for k in range(4)
            for j in range(2)
        ]
    )
    x_own = lax.dynamic_slice_in_dim(images, starts[0], 64, 0).astype(F32)
    g_own = lax.dynamic_slice_in_dim(cotangent, starts[0], 64, 0).astype(F32)
    x_hat_own, x_std_own = normalize(x_own)

    w_mine = jnp.concatenate(gather_half(w_out.astype(F32)))
    a, q, k, v, lse, ctx32, ctx_t = attn_forward(
        starts, images, w_qkv, bias_query, bias_value, norm1_gain, norm1_shift
    )
    w_full = round_weights(w_mine, from_core(w_mine))
    gm = grad_rows(starts, cotangent, scale_mlp)

    attn, hmid, b_hat, b_std, b_own = middle(
        heads_to_rows(ctx32), w_full, x_own, bias_out, scale_attn, norm2_gain, norm2_shift
    )
    gb_part, b, act, gpre, sum_gpre = mlp(gather_rows(b_own), gm, w_up, w_down, bias_up)
    gb = scatter_rows(gb_part)
    mlp_part = mm(act, w_down)
    ff = lax.psum_scatter(
        jnp.concatenate([tmm(b, gpre), tmm(gm, act)], axis=1),
        DATA,
        scatter_dimension=0,
        tiled=True,
    )

    gh = g_own + norm_back(gb, b_hat, b_std, norm2_gain)
    ga32 = gh * scale_attn
    ga_own = ga32.astype(BF)
    gctx = rows_to_heads(mmt(ga_own, w_full))

    mlp_out = scatter_rows(mlp_part) + bias_down
    final = hmid + scale_mlp * mlp_out

    g_mixed = attn_backward(q, k, v, lse, gctx)
    ga_part, norm1_sums, sum_mixed = input_grad(starts, images, g_mixed, w_qkv)
    g_norm1 = scatter_rows(ga_part)
    grad_in = gh + norm_back(g_norm1, x_hat_own, x_std_own, norm1_gain)

    grad_out = out_grad(ctx_t, gather_rows(ga32))
    at = lax.psum_scatter(
        jnp.concatenate([tmm(a, g_mixed), grad_out], axis=1),
        DATA,
        scatter_dimension=0,
        tiled=True,
    )

    wide = jnp.concatenate(
        [
            rows(ga_own.astype(F32)),
            rows(gm[:64].astype(F32)),
            norm1_sums,
            rows(gb * b_hat),
            rows(gb),
            rows(gh * attn),
            rows(g_own * mlp_out),
        ]
    )
    for axis, size in (("c", 2), ("z", 4), ("yh", 2)):
        wide = butterfly(wide, axis, size)
    narrow = jnp.concatenate(
        [sum_mixed[:, :64], sum_mixed[:, 128:], sum_gpre, jnp.zeros((1, 640), F32)], axis=1
    )
    sums = jnp.concatenate([wide, jnp.broadcast_to(narrow, (8, 1024))])
    for axis, size in (("yl", 2), ("x", 4)):
        sums = butterfly(sums, axis, size)

    def absolute(own):
        half = gather_half(own)
        other = from_core(jnp.concatenate(half))
        out = jnp.zeros((1024, 1024), F32)
        for n in range(8):
            out = lax.dynamic_update_slice_in_dim(out, half[n], starts[n], 0)
        for n in range(8):
            out = lax.dynamic_update_slice_in_dim(
                out, other[n * 64 : n * 64 + 64], starts[8 + n], 0
            )
        return out[None]

    return (
        absolute(final),
        absolute(grad_in),
        at[None, :, :192],
        sums[8:9, :64],
        sums[8:9, 64:128],
        at[:, 192:].T[None],
        sums[0:1],
        ff[None, :, :256],
        sums[8:9, 128:384],
        ff[:, 256:].T[None],
        sums[1:2],
        sums[2:3],
        sums[3:4],
        sums[4:5],
        sums[5:6],
        sums[6:7],
        sums[7:8],
    )


def solution(mesh):
    fine = Mesh(mesh.devices.reshape(2, 4, 4, 2, 2), ("yl", "x", "z", "yh", "c"))
    return jax.shard_map(
        on_device,
        mesh=fine,
        in_specs=(
            P(DATA, None, None),
            P(None, None, TENSOR),
            P(None, TENSOR),
            P(None, TENSOR),
            P(None, TENSOR, None),
            P(),
            P(None, None, TENSOR),
            P(None, TENSOR),
            P(None, TENSOR, None),
            P(),
            P(),
            P(),
            P(),
            P(),
            P(),
            P(),
            P(DATA, None, None),
        ),
        out_specs=(
            P(DATA, None, None),
            P(DATA, None, None),
            P(None, DATA, TENSOR),
            P(None, TENSOR),
            P(None, TENSOR),
            P(None, TENSOR, DATA),
            P(),
            P(None, DATA, TENSOR),
            P(None, TENSOR),
            P(None, TENSOR, DATA),
            P(),
            P(),
            P(),
            P(),
            P(),
            P(),
            P(),
        ),
        check_vma=False,
    )
```

```python
import jax
import jax.numpy as jnp
from jax import lax
from jax.experimental import pallas as pl
from jax.experimental.pallas import tpu as pltpu
from jax.sharding import Mesh, PartitionSpec as P

DH = 64
EPS = 1e-06
BF = jnp.bfloat16
F32 = jnp.float32
DATA = ("yl", "x")
TENSOR = ("z", "yh", "c")
CHIPS = ("z", "yh")
FACTOR = DH ** (-0.5)
VMEM_BYTES = 20 * 1024 * 1024


def from_core(v):
    return lax.ppermute(v, "c", [(0, 1), (1, 0)])


def from_yh(v):
    return lax.ppermute(v, "yh", [(0, 1), (1, 0)])


def from_z(v, k):
    return lax.ppermute(v, "z", [((i + k) % 4, i) for i in range(4)])


def hold(values, *tokens):
    return lax.optimization_barrier((values, tokens))[0]


GATHERED = ((0, 0), (0, 1), (1, 0), (1, 1), (2, 0), (3, 0), (4, 0), (4, 1))
PARTIAL = ((0, 0), (1, 0), (2, 0), (2, 1), (3, 0), (4, 0), (5, 0), (5, 1))


def gather_near(s):
    return s, from_yh(s), from_z(s, 2)


def gather_far(s, y, a2):
    own = jnp.concatenate([s, y])
    return [own, from_z(own, 1), a2, from_yh(a2), from_z(own, 3)]


def gather_core(half):
    return list(half) + [from_core(piece) for piece in half]


def scatter_core(pieces):
    return [from_core(piece) for piece in pieces[6:]]


def scatter_add(pieces, got):
    return [mine + other for mine, other in zip(pieces[:6], got)]


def scatter_near(u):
    m, my, p1, p2, p2y, p3 = u
    return from_yh(p2y), from_z(p1, 3), from_z(p3, 1)


def scatter_join(u, near):
    m, my, p1, p2, p2y, p3 = u
    r2y, r1, r3 = near
    return p2 + r2y, my + r1[64:] + r3[64:]


def scatter_far(q):
    return from_z(q[0], 2), from_yh(q[1])


def scatter_end(u, near, far):
    return u[0] + near[1][:64] + near[2][:64] + far[0] + far[1]


def swap_chips(blocks):
    return lax.all_to_all(blocks, CHIPS, 0, 0, tiled=True)


def sum_images(*blocks):
    both = jnp.concatenate(blocks, axis=1)
    return lax.psum_scatter(both, "x", scatter_dimension=0, tiled=True)


def halves(v, upper):
    n = v.shape[1] // 2
    return jnp.where(upper, v[:, n:], v[:, :n])


def pair_sum(v, axis):
    return v + lax.ppermute(v, axis, [(0, 1), (1, 0)])


def ring_sum(v, axis):
    got = [lax.ppermute(v, axis, [((i + k) % 4, i) for i in range(4)]) for k in (1, 2, 3)]
    return (v + got[1]) + (got[0] + got[2])


def normalize(values):
    centre = jnp.mean(values, axis=-1, keepdims=True)
    shifted = values - centre
    spread = jnp.mean(shifted * shifted, axis=-1, keepdims=True)
    inv_std = lax.rsqrt(spread + EPS)
    return shifted * inv_std, inv_std


def norm_back(grad_normed, x_hat, inv_std, gain):
    grad_hat = grad_normed * gain
    first = jnp.mean(grad_hat, axis=-1, keepdims=True)
    second = jnp.mean(grad_hat * x_hat, axis=-1, keepdims=True)
    return inv_std * (grad_hat - first - x_hat * second)


def mm(a, b):
    return jnp.dot(a, b, preferred_element_type=F32)


def mmt(a, b):
    return lax.dot_general(a, b, (((1,), (1,)), ((), ())), preferred_element_type=F32)


def tmm(a, b):
    return lax.dot_general(a, b, (((0,), (0,)), ((), ())), preferred_element_type=F32)


def rows(v):
    return jnp.sum(v, axis=0, keepdims=True)


def shape(dims, dtype=F32):
    return jax.ShapeDtypeStruct(dims, dtype)


PARTIAL_PIECES = tuple(shape((r, 1024)) for r in (64, 64, 128, 64, 64, 128)) * 2
ON_CHIP = pl.BlockSpec(memory_space=pltpu.VMEM)
SCALARS = pl.BlockSpec(memory_space=pltpu.SMEM)


def params():
    return pltpu.CompilerParams(vmem_limit_bytes=VMEM_BYTES)


def cost(us):
    return pl.CostEstimate(
        flops=int(us * 5e8), bytes_accessed=int(us * 3e6), transcendentals=0
    )


def gathered(refs, n):
    piece, part = GATHERED[n % 8]
    return refs[5 * (n // 8) + piece].at[pl.ds(part * 64, 64)]


def put_partial(refs, n, values):
    piece, part = PARTIAL[n % 8]
    refs[6 * (n // 8) + piece][part * 64 : part * 64 + 64] = values


def local_call(body, name, us, out_shape, *args, scratch=()):
    return pl.pallas_call(
        body,
        out_shape=out_shape,
        in_specs=[SCALARS if v.dtype == jnp.int32 else ON_CHIP for v in args],
        out_specs=jax.tree.map(lambda _: ON_CHIP, out_shape),
        scratch_shapes=list(scratch),
        compiler_params=params(),
        cost_estimate=cost(us),
        name=name,
    )(*args)


def attn_forward_kernel(
    starts, x, w, bq, bv, gain, shift, a, q, k, v, lse, ctx_mine, ctx_other, ctx_t, v_t
):
    gain_v, shift_v = gain[...], shift[...]
    for n in range(8):
        lo, hi = starts[2 * n], starts[2 * n + 1]
        rows_n = jnp.concatenate(
            [x[pl.ds(pl.multiple_of(lo, 64), 64)], x[pl.ds(pl.multiple_of(hi, 64), 64)]]
        ).astype(F32)
        x_hat, _ = normalize(rows_n)
        a_n = (x_hat * gain_v + shift_v).astype(BF)
        here = pl.ds(n * 128, 128)
        a[here] = a_n
        mixed = mm(a_n, w[...])
        q[here] = (mixed[:, :64] + bq[...]).astype(BF)
        k[here] = mixed[:, 64:128].astype(BF)
        v_n = (mixed[:, 128:] + bv[...]).astype(BF)
        v[here] = v_n
        v_t[:, here] = v_n.astype(F32).T.astype(BF)
    for n in range(4):
        here = pl.ds(n * 256, 256)
        scores = mmt(k[...], q[here]) * FACTOR
        peak = jnp.max(scores, axis=0, keepdims=True)
        expo = jnp.exp(scores - peak)
        denom = jnp.sum(expo, axis=0, keepdims=True)
        probs = (expo / denom).astype(BF)
        lse[:, here] = peak + jnp.log(denom)
        ctx = mm(v_t[...], probs)
        ctx_t[:, here] = ctx.astype(BF)
        ctx = ctx.T
        half = ctx_mine if n < 2 else ctx_other
        for m in range(4):
            at = pl.multiple_of(lax.rem(starts[4 * n + m], 512), 64)
            half[pl.ds(at, 64)] = ctx[m * 64 : m * 64 + 64]


def attn_forward(*args):
    small = shape((1024, 64), BF)
    part = shape((512, 64))
    return local_call(
        attn_forward_kernel,
        "attn_forward",
        6,
        (
            shape((1024, 1024), BF),
            small,
            small,
            small,
            shape((1, 1024)),
            part,
            part,
            shape((64, 1024), BF),
        ),
        *args,
        scratch=[pltpu.VMEM((64, 1024), BF)],
    )


def grad_rows_kernel(starts, g, scale, gm):
    gm[...] = (g[...].astype(F32) * scale[...]).astype(BF)


def grad_rows(starts, cotangent, scale):
    return pl.pallas_call(
        grad_rows_kernel,
        out_shape=shape((1024, 1024), BF),
        grid_spec=pltpu.PrefetchScalarGridSpec(
            num_scalar_prefetch=1,
            grid=(16,),
            in_specs=[
                pl.BlockSpec((64, 1024), lambda n, s: (s[n] // 64, 0)),
                pl.BlockSpec((1, 1024), lambda n, s: (0, 0)),
            ],
            out_specs=pl.BlockSpec((64, 1024), lambda n, s: (n, 0)),
        ),
        compiler_params=params(),
        cost_estimate=cost(1.5),
        name="grad_rows",
    )(starts, cotangent, scale)


def round_weights_kernel(starts, *refs):
    out = refs[10]
    for i in range(2):
        for n in range(8):
            at = lax.rem(starts[n], 512) * 2 + i * 64
            out[pl.ds(pl.multiple_of(at, 64), 64)] = gathered(refs, 8 * i + n)[...].astype(BF)


def round_weights(starts, pieces):
    return local_call(
        round_weights_kernel, "round_weights", 3, shape((1024, 1024), BF), starts, *pieces
    )


def middle_kernel(ctx, w, x, bias, scale, gain, shift, attn, hmid, b_hat, b_std, b):
    c = jnp.concatenate([ctx[n] for n in range(8)], axis=1).astype(BF)
    y = mm(c, w[...]) + bias[...]
    attn[...] = y
    h = x[...] + scale[...] * y
    hmid[...] = h
    hat, std = normalize(h)
    b_hat[...] = hat
    b_std[...] = std
    b[...] = hat * gain[...] + shift[...]


def middle(*args):
    wide = shape((64, 1024))
    return local_call(
        middle_kernel, "middle", 1, (wide, wide, wide, shape((64, 1)), wide), *args
    )


def mlp_kernel(*refs):
    b32, (gm, w_up, w_down, bias), gb = refs[:10], refs[10:14], refs[14:26]
    b, act, gpre, total = refs[26:]
    count = jnp.zeros((1, 256), F32)
    for n in (2, 3, 0, 1):
        here = pl.ds(n * 256, 256)
        b_n = jnp.concatenate([gathered(b32, 4 * n + m)[...] for m in range(4)]).astype(BF)
        b[here] = b_n
        pre = mm(b_n, w_up[...]) + bias[...]
        cdf = 0.5 * (1.0 + lax.erf(pre * (0.5**0.5)))
        act[here] = (pre * cdf).astype(BF)
        slope = cdf + pre * (jnp.exp(-0.5 * pre * pre) * 0.3989422804014327)
        gpre_n = (mmt(gm[here], w_down[...]) * slope).astype(BF)
        gpre[here] = gpre_n
        back = mmt(gpre_n, w_up[...])
        for m in range(4):
            put_partial(gb, 4 * n + m, back[m * 64 : m * 64 + 64])
        count += rows(gpre_n.astype(F32))
    total[...] = count


def mlp(pieces, *args):
    out = local_call(
        mlp_kernel,
        "mlp",
        8,
        PARTIAL_PIECES
        + (
            shape((1024, 1024), BF),
            shape((1024, 256), BF),
            shape((1024, 256), BF),
            shape((1, 256)),
        ),
        *pieces,
        *args,
    )
    return out[:12], *out[12:]


def mlp_down_kernel(starts, act, w, g, bias, *refs):
    out, scale_sum = refs[:12], refs[12]
    total = bias[...] * rows(g[pl.ds(pl.multiple_of(starts[0], 64), 64)].astype(F32))
    for n in range(4):
        y = mm(act[pl.ds(n * 256, 256)], w[...])
        for m in range(4):
            y_m = y[m * 64 : m * 64 + 64]
            put_partial(out, 4 * n + m, y_m)
            at = pl.multiple_of(starts[4 * n + m], 64)
            total += rows(y_m * g[pl.ds(at, 64)].astype(F32))
    scale_sum[...] = total


def mlp_down(*args):
    out = local_call(
        mlp_down_kernel, "mlp_down", 3, PARTIAL_PIECES + (shape((1, 1024)),), *args
    )
    return out[:12], out[12]


def grad_middle_kernel(
    gb, hat, std, gain, g, attn, scale, w, gh, ga32, blocks, sums
):
    gb_v, hat_v = gb[...], hat[...]
    gh_v = g[...] + norm_back(gb_v, hat_v, std[...], gain[...])
    gh[...] = gh_v
    ga_v = gh_v * scale[...]
    ga32[...] = ga_v
    ga = ga_v.astype(BF)
    y = mmt(ga, w[...])
    for n in range(8):
        blocks[n] = y[:, n * 128 : n * 128 + 128]
    sums[0:1] = rows(ga.astype(F32))
    sums[1:2] = rows(gb_v * hat_v)
    sums[2:3] = rows(gb_v)
    sums[3:4] = rows(gh_v * attn[...])


def grad_middle(*args):
    wide = shape((64, 1024))
    return local_call(
        grad_middle_kernel,
        "grad_middle",
        1.5,
        (wide, wide, shape((8, 64, 128)), shape((4, 1024))),
        *args,
    )


def attn_backward_kernel(starts, q, k, v, lse, mine, other, mixed, gq_t, g):
    for n in range(16):
        at = pl.ds(pl.multiple_of(lax.rem(starts[n], 512), 64), 64)
        block = mine[at, :64] if n < 8 else other[at]
        g[n * 64 : n * 64 + 64] = block.astype(BF)
    k_t = k[...].astype(F32).T.astype(BF)
    gk = jnp.zeros((1024, 64), F32)
    gv = jnp.zeros((1024, 64), F32)
    for n in range(4):
        here = pl.ds(n * 256, 256)
        gctx_n = g[here]
        q_n = q[here]
        p = jnp.exp(mmt(k[...], q_n) * FACTOR - lse[:, here])
        gv += mm(p.astype(BF), gctx_n)
        gp = mmt(v[...], gctx_n)
        gs = (p * (gp - jnp.sum(p * gp, axis=0, keepdims=True))).astype(BF)
        gk += mm(gs, q_n)
        gq_t[:, here] = mm(k_t, gs)
    mixed[...] = jnp.concatenate([gq_t[...].T * FACTOR, gk * FACTOR, gv], axis=1).astype(BF)


def attn_backward(*args):
    return local_call(
        attn_backward_kernel,
        "attn_backward",
        6,
        shape((1024, 192), BF),
        *args,
        scratch=[pltpu.VMEM((64, 1024), F32), pltpu.VMEM((1024, 64), BF)],
    )


def input_grad_kernel(starts, x, mixed, w, *refs):
    out, (sums, cols) = refs[:12], refs[12:]
    gain_sum = jnp.zeros((1, 1024), F32)
    shift_sum = jnp.zeros((1, 1024), F32)
    for n in (4, 5, 6, 7, 0, 1, 2, 3):
        lo, hi = starts[2 * n], starts[2 * n + 1]
        x_n = jnp.concatenate(
            [x[pl.ds(pl.multiple_of(lo, 64), 64)], x[pl.ds(pl.multiple_of(hi, 64), 64)]]
        ).astype(F32)
        x_hat, _ = normalize(x_n)
        y = mmt(mixed[pl.ds(n * 128, 128)], w[...])
        put_partial(out, 2 * n, y[:64])
        put_partial(out, 2 * n + 1, y[64:])
        gain_sum += rows(y * x_hat)
        shift_sum += rows(y)
    sums[0:1] = gain_sum
    sums[1:2] = shift_sum
    cols[...] = rows(mixed[...].astype(F32))


def input_grad(*args):
    out = local_call(
        input_grad_kernel,
        "input_grad",
        6,
        PARTIAL_PIECES + (shape((2, 1024)), shape((1, 192))),
        *args,
    )
    return out[:12], *out[12:]


def out_grad_kernel(starts, ctx_t, mine, other, out, ga):
    for n in range(16):
        at = lax.rem(starts[n], 512) // 128 * 128 + (n % 2) * 64
        half = mine if n < 8 else other
        ga[n * 64 : n * 64 + 64] = half[pl.ds(pl.multiple_of(at, 64), 64)].astype(BF)
    y = mm(ctx_t[...], ga[...])
    for n in range(8):
        x, yl = n % 4, n // 4
        out[x * 64 : x * 64 + 64, yl * 128 : yl * 128 + 128] = y[:, n * 128 : n * 128 + 128]


def out_grad(*args):
    return local_call(
        out_grad_kernel,
        "out_grad",
        3,
        shape((256, 256)),
        *args,
        scratch=[pltpu.VMEM((1024, 1024), BF)],
    )


def last_rows_kernel(g, x, gain, gh, out):
    hat, std = normalize(x[...])
    out[...] = gh[...] + norm_back(g[...], hat, std, gain[...])


def last_rows(*args):
    return local_call(last_rows_kernel, "last_rows", 0.5, shape((64, 1024)), *args)


def place_kernel(starts, *refs):
    pieces, out, sems = refs[:10], refs[10], refs[11]
    copies = []
    for n in range(16):
        at = pl.multiple_of(starts[n], 64)
        copies.append(
            pltpu.make_async_copy(gathered(pieces, n), out.at[pl.ds(at, 64)], sems.at[n])
        )
    for copy in copies:
        copy.start()
    for copy in copies:
        copy.wait()


def place(starts, pieces):
    return pl.pallas_call(
        place_kernel,
        out_shape=shape((1024, 1024)),
        in_specs=[SCALARS] + [ON_CHIP] * 10,
        out_specs=pl.BlockSpec(memory_space=pl.ANY),
        scratch_shapes=[pltpu.SemaphoreType.DMA((16,))],
        compiler_params=params(),
        cost_estimate=cost(3),
        name="place",
    )(starts, *pieces)


def on_device(
    images,
    w_qkv,
    bias_query,
    bias_value,
    w_out,
    bias_out,
    w_up,
    bias_up,
    w_down,
    bias_down,
    norm1_gain,
    norm1_shift,
    norm2_gain,
    norm2_shift,
    scale_attn,
    scale_mlp,
    cotangent,
):
    w_qkv, w_out, w_up, w_down = w_qkv[0], w_out[0], w_up[0], w_down[0]
    images, cotangent = images[0], cotangent[0]
    c, z, yh = lax.axis_index("c"), lax.axis_index("z"), lax.axis_index("yh")
    starts = jnp.stack(
        [
            (((c + i) % 2) * 8 + ((z + k) % 4) * 2 + ((yh + j) % 2)) * 64
            for i in range(2)
            for k in range(4)
            for j in range(2)
        ]
    )
    x_own = lax.dynamic_slice_in_dim(images, starts[0], 64, 0).astype(F32)
    g_own = lax.dynamic_slice_in_dim(cotangent, starts[0], 64, 0).astype(F32)

    w_near = hold(gather_near(w_out.astype(F32)))
    w_half = gather_far(*w_near)
    a, q, k, v, lse, ctx_mine, ctx_other, ctx_t = attn_forward(
        starts,
        hold(images, w_near),
        w_qkv,
        bias_query,
        bias_value,
        norm1_gain,
        norm1_shift,
    )
    pair = jnp.concatenate([ctx_mine, from_core(ctx_other)], axis=1)
    ctx_own = swap_chips(pair.reshape(8, 64, 128))
    w_full = round_weights(starts, gather_core(hold(w_half, pair)))
    attn, hmid, b_hat, b_std, b_own = middle(
        ctx_own, w_full, x_own, bias_out, scale_attn, norm2_gain, norm2_shift
    )
    b_near = gather_near(b_own)
    gm = grad_rows(starts, hold(cotangent, b_own), scale_mlp)
    b_half = gather_far(*hold(b_near))
    gb_part, b, act, gpre, sum_gpre = mlp(gather_core(b_half), gm, w_up, w_down, bias_up)

    gb_u = hold(scatter_add(gb_part, scatter_core(gb_part)))
    gb_near = hold(scatter_near(gb_u))
    act, gpre = hold((act, gpre), gb_u)
    mlp_part, scale_sum = mlp_down(starts, act, w_down, cotangent, bias_down)
    gb_q = hold(scatter_join(gb_u, gb_near))
    mlp_got = hold(scatter_core(mlp_part), gb_q)
    mlp_u = scatter_add(mlp_part, mlp_got)
    gb = scatter_end(gb_u, gb_near, hold(scatter_far(gb_q), mlp_u))
    gh, ga32, gctx_blocks, mid_sums = grad_middle(
        gb, b_hat, b_std, norm2_gain, g_own, attn, scale_attn, w_full
    )
    mlp_near = scatter_near(hold(mlp_u, gctx_blocks))
    ga_other = from_yh(ga32)
    gctx = swap_chips(gctx_blocks).reshape(512, 128)
    gctx_other = from_core(gctx[:, 64:])
    ga_other, mlp_near, gctx = hold((ga_other, mlp_near, gctx))
    mlp_far = scatter_far(scatter_join(mlp_u, mlp_near))
    ga_half = lax.all_gather(jnp.concatenate([ga32, ga_other]), "z", axis=0, tiled=True)
    g_mixed = attn_backward(starts, q, k, v, lse, gctx, gctx_other)

    ga_part, norm1_sums, sum_mixed = input_grad(starts, images, g_mixed, w_qkv)
    vectors = jnp.concatenate([mid_sums, rows(gm[:64].astype(F32)), norm1_sums, scale_sum])
    vectors = pair_sum(vectors, "c")
    in_u, vectors = hold((scatter_add(ga_part, scatter_core(ga_part)), vectors))
    in_near = scatter_near(in_u)
    vectors = ring_sum(vectors, "z")
    ga_half = hold(ga_half, in_u)
    grad_out = out_grad(starts, ctx_t, ga_half, from_core(ga_half))

    in_near, vectors, grad_out, mlp_far = hold((in_near, vectors, grad_out, mlp_far))
    in_far = scatter_far(scatter_join(in_u, in_near))
    mlp_out = scatter_end(mlp_u, mlp_near, mlp_far) + bias_down
    final = hmid + scale_mlp * mlp_out
    final_near = gather_near(final)
    vectors = pair_sum(vectors, "yh")
    in_far, vectors, final_near = hold((in_far, vectors, final_near))
    g_norm1 = scatter_end(in_u, in_near, in_far)
    grad_in = last_rows(g_norm1, x_own, norm1_gain, gh)

    end_near = gather_near(grad_in)
    final_half = gather_far(*final_near)
    narrow = jnp.concatenate(
        [sum_mixed[:, :64], sum_mixed[:, 128:], sum_gpre, jnp.zeros((1, 640), F32)], axis=1
    )
    sums = jnp.concatenate([vectors, jnp.broadcast_to(narrow, (8, 1024))])
    sums = pair_sum(sums, "yl")
    left, right = slice(0, 512), slice(512, 1024)
    up_x = sum_images(tmm(b[:, left], gpre), tmm(b[:, right], gpre))
    down_x = sum_images(tmm(gm[:, left], act), tmm(gm[:, right], act))
    a_late = hold(a, in_u)
    qkv_x = sum_images(tmm(a_late[:, left], g_mixed), tmm(a_late[:, right], g_mixed))
    out_x = sum_images(grad_out)
    end_near, sums, up_x, down_x, qkv_x, out_x = hold(
        (end_near, sums, up_x, down_x, qkv_x, out_x)
    )
    end_half = gather_far(*end_near)
    sums = ring_sum(sums, "x")
    upper = lax.axis_index("yl") == 1
    grad_up, grad_down, grad_qkv, grad_out = (
        halves(v, upper) + lax.ppermute(halves(v, ~upper), "yl", [(0, 1), (1, 0)])
        for v in (up_x, down_x, qkv_x, out_x)
    )
    final_all = place(starts, gather_core(final_half))
    end_half, sums, grad_up, grad_down, grad_qkv, grad_out, final_all = hold(
        (end_half, sums, grad_up, grad_down.T, grad_qkv, grad_out, final_all)
    )
    grad_input = place(starts, gather_core(end_half))

    return (
        final_all[None],
        grad_input[None],
        grad_qkv[None],
        sums[8:9, :64],
        sums[8:9, 64:128],
        grad_out[None],
        sums[0:1],
        grad_up[None],
        sums[8:9, 128:384],
        grad_down[None],
        sums[4:5],
        sums[5:6],
        sums[6:7],
        sums[1:2],
        sums[2:3],
        sums[3:4],
        sums[7:8],
    )


def solution(mesh):
    fine = Mesh(mesh.devices.reshape(2, 4, 4, 2, 2), ("yl", "x", "z", "yh", "c"))
    return jax.shard_map(
        on_device,
        mesh=fine,
        in_specs=(
            P(DATA, None, None),
            P(None, None, TENSOR),
            P(None, TENSOR),
            P(None, TENSOR),
            P(None, TENSOR, None),
            P(),
            P(None, None, TENSOR),
            P(None, TENSOR),
            P(None, TENSOR, None),
            P(),
            P(),
            P(),
            P(),
            P(),
            P(),
            P(),
            P(DATA, None, None),
        ),
        out_specs=(
            P(DATA, None, None),
            P(DATA, None, None),
            P(None, DATA, TENSOR),
            P(None, TENSOR),
            P(None, TENSOR),
            P(None, TENSOR, DATA),
            P(),
            P(None, DATA, TENSOR),
            P(None, TENSOR),
            P(None, TENSOR, DATA),
            P(),
            P(),
            P(),
            P(),
            P(),
            P(),
            P(),
        ),
        check_vma=False,
    )
```

```python
import jax
import jax.numpy as jnp
from jax import lax
from jax.experimental import pallas as pl
from jax.experimental.pallas import tpu as pltpu
from jax.sharding import Mesh, PartitionSpec as P

DH = 64
EPS = 1e-06
BF = jnp.bfloat16
F32 = jnp.float32
DATA = ("yl", "x")
TENSOR = ("z", "yh", "c")
CHIPS = ("z", "yh")
FACTOR = DH ** (-0.5)
VMEM_BYTES = 20 * 1024 * 1024


def from_core(v):
    return lax.ppermute(v, "c", [(0, 1), (1, 0)])


def from_yh(v):
    return lax.ppermute(v, "yh", [(0, 1), (1, 0)])


def from_z(v, k):
    return lax.ppermute(v, "z", [((i + k) % 4, i) for i in range(4)])


def hold(values, *tokens):
    return lax.optimization_barrier((values, tokens))[0]


GATHERED = ((0, 0), (0, 1), (1, 0), (1, 1), (2, 0), (3, 0), (4, 0), (4, 1))
PARTIAL = ((0, 0), (1, 0), (2, 0), (2, 1), (3, 0), (4, 0), (5, 0), (5, 1))


def gather_near(s):
    return s, from_yh(s), from_z(s, 2)


def gather_far(s, y, a2):
    own = jnp.concatenate([s, y])
    return [own, from_z(own, 1), a2, from_yh(a2), from_z(own, 3)]


def gather_core(half):
    return list(half) + [from_core(piece) for piece in half]


def scatter_core(pieces):
    return [from_core(piece) for piece in pieces[6:]]


def scatter_add(pieces, got):
    return [mine + other for mine, other in zip(pieces[:6], got)]


def scatter_near(u):
    m, my, p1, p2, p2y, p3 = u
    return from_yh(p2y), from_z(p1, 3), from_z(p3, 1)


def scatter_join(u, near):
    m, my, p1, p2, p2y, p3 = u
    r2y, r1, r3 = near
    return p2 + r2y, my + r1[64:] + r3[64:]


def scatter_far(q):
    return from_z(q[0], 2), from_yh(q[1])


def scatter_end(u, near, far):
    return u[0] + near[1][:64] + near[2][:64] + far[0] + far[1]


def swap_chips(blocks):
    return lax.all_to_all(blocks, CHIPS, 0, 0, tiled=True)


def sum_images(*blocks):
    both = jnp.concatenate(blocks, axis=1)
    return lax.psum_scatter(both, "x", scatter_dimension=0, tiled=True)


def halves(v, upper):
    n = v.shape[1] // 2
    return jnp.where(upper, v[:, n:], v[:, :n])


def pair_sum(v, axis):
    return v + lax.ppermute(v, axis, [(0, 1), (1, 0)])


def ring_sum(v, axis):
    got = [lax.ppermute(v, axis, [((i + k) % 4, i) for i in range(4)]) for k in (1, 2, 3)]
    return (v + got[1]) + (got[0] + got[2])


def normalize(values):
    centre = jnp.mean(values, axis=-1, keepdims=True)
    shifted = values - centre
    spread = jnp.mean(shifted * shifted, axis=-1, keepdims=True)
    inv_std = lax.rsqrt(spread + EPS)
    return shifted * inv_std, inv_std


def norm_back(grad_normed, x_hat, inv_std, gain):
    grad_hat = grad_normed * gain
    first = jnp.mean(grad_hat, axis=-1, keepdims=True)
    second = jnp.mean(grad_hat * x_hat, axis=-1, keepdims=True)
    return inv_std * (grad_hat - first - x_hat * second)


def mm(a, b):
    return jnp.dot(a, b, preferred_element_type=F32)


def mmt(a, b):
    return lax.dot_general(a, b, (((1,), (1,)), ((), ())), preferred_element_type=F32)


def tmm(a, b):
    return lax.dot_general(a, b, (((0,), (0,)), ((), ())), preferred_element_type=F32)


def rows(v):
    return jnp.sum(v, axis=0, keepdims=True)


def shape(dims, dtype=F32):
    return jax.ShapeDtypeStruct(dims, dtype)


PARTIAL_PIECES = tuple(shape((r, 1024)) for r in (64, 64, 128, 64, 64, 128)) * 2
ON_CHIP = pl.BlockSpec(memory_space=pltpu.VMEM)
SCALARS = pl.BlockSpec(memory_space=pltpu.SMEM)


def params():
    return pltpu.CompilerParams(vmem_limit_bytes=VMEM_BYTES)


def cost(us):
    return pl.CostEstimate(
        flops=int(us * 5e8), bytes_accessed=int(us * 3e6), transcendentals=0
    )


def gathered(refs, n):
    piece, part = GATHERED[n % 8]
    return refs[5 * (n // 8) + piece].at[pl.ds(part * 64, 64)]


def put_partial(refs, n, values):
    piece, part = PARTIAL[n % 8]
    refs[6 * (n // 8) + piece][part * 64 : part * 64 + 64] = values


def local_call(body, name, us, out_shape, *args, scratch=()):
    return pl.pallas_call(
        body,
        out_shape=out_shape,
        in_specs=[SCALARS if v.dtype == jnp.int32 else ON_CHIP for v in args],
        out_specs=jax.tree.map(lambda _: ON_CHIP, out_shape),
        scratch_shapes=list(scratch),
        compiler_params=params(),
        cost_estimate=cost(us),
        name=name,
    )(*args)


def attn_forward_kernel(
    starts, x, w, bq, bv, gain, shift, a, q, k, v, lse, ctx_mine, ctx_other, ctx_t, v_t
):
    gain_v, shift_v = gain[...], shift[...]
    for n in range(8):
        lo, hi = starts[2 * n], starts[2 * n + 1]
        rows_n = jnp.concatenate(
            [x[pl.ds(pl.multiple_of(lo, 64), 64)], x[pl.ds(pl.multiple_of(hi, 64), 64)]]
        ).astype(F32)
        x_hat, _ = normalize(rows_n)
        a_n = (x_hat * gain_v + shift_v).astype(BF)
        here = pl.ds(n * 128, 128)
        a[here] = a_n
        mixed = mm(a_n, w[...])
        q[here] = (mixed[:, :64] + bq[...]).astype(BF)
        k[here] = mixed[:, 64:128].astype(BF)
        v_n = (mixed[:, 128:] + bv[...]).astype(BF)
        v[here] = v_n
        v_t[:, here] = v_n.astype(F32).T.astype(BF)
    for n in range(4):
        here = pl.ds(n * 256, 256)
        scores = mmt(k[...], q[here]) * FACTOR
        peak = jnp.max(scores, axis=0, keepdims=True)
        expo = jnp.exp(scores - peak)
        denom = jnp.sum(expo, axis=0, keepdims=True)
        probs = (expo / denom).astype(BF)
        lse[:, here] = peak + jnp.log(denom)
        ctx = mm(v_t[...], probs)
        ctx_t[:, here] = ctx.astype(BF)
        ctx = ctx.T
        half = ctx_mine if n < 2 else ctx_other
        for m in range(4):
            at = pl.multiple_of(lax.rem(starts[4 * n + m], 512), 64)
            half[pl.ds(at, 64)] = ctx[m * 64 : m * 64 + 64]


def attn_forward(*args):
    small = shape((1024, 64), BF)
    part = shape((512, 64))
    return local_call(
        attn_forward_kernel,
        "attn_forward",
        6,
        (
            shape((1024, 1024), BF),
            small,
            small,
            small,
            shape((1, 1024)),
            part,
            part,
            shape((64, 1024), BF),
        ),
        *args,
        scratch=[pltpu.VMEM((64, 1024), BF)],
    )


def grad_rows_kernel(starts, g, scale, gm):
    gm[...] = (g[...].astype(F32) * scale[...]).astype(BF)


def grad_rows(starts, cotangent, scale):
    return pl.pallas_call(
        grad_rows_kernel,
        out_shape=shape((1024, 1024), BF),
        grid_spec=pltpu.PrefetchScalarGridSpec(
            num_scalar_prefetch=1,
            grid=(16,),
            in_specs=[
                pl.BlockSpec((64, 1024), lambda n, s: (s[n] // 64, 0)),
                pl.BlockSpec((1, 1024), lambda n, s: (0, 0)),
            ],
            out_specs=pl.BlockSpec((64, 1024), lambda n, s: (n, 0)),
        ),
        compiler_params=params(),
        cost_estimate=cost(1.5),
        name="grad_rows",
    )(starts, cotangent, scale)


def round_weights_kernel(starts, *refs):
    out = refs[10]
    for i in range(2):
        for n in range(8):
            at = lax.rem(starts[n], 512) * 2 + i * 64
            out[pl.ds(pl.multiple_of(at, 64), 64)] = gathered(refs, 8 * i + n)[...].astype(BF)


def round_weights(starts, pieces):
    return local_call(
        round_weights_kernel, "round_weights", 3, shape((1024, 1024), BF), starts, *pieces
    )


def middle_kernel(ctx, w, x, bias, scale, gain, shift, attn, hmid, b_hat, b_std, b):
    c = jnp.concatenate([ctx[n] for n in range(8)], axis=1).astype(BF)
    y = mm(c, w[...]) + bias[...]
    attn[...] = y
    h = x[...] + scale[...] * y
    hmid[...] = h
    hat, std = normalize(h)
    b_hat[...] = hat
    b_std[...] = std
    b[...] = hat * gain[...] + shift[...]


def middle(*args):
    wide = shape((64, 1024))
    return local_call(
        middle_kernel, "middle", 1, (wide, wide, wide, shape((64, 1)), wide), *args
    )


def mlp_kernel(*refs):
    b32, (gm, w_up, w_down, bias), gb = refs[:10], refs[10:14], refs[14:26]
    b, act, gpre, total = refs[26:]
    count = jnp.zeros((1, 256), F32)
    for n in (2, 3, 0, 1):
        here = pl.ds(n * 256, 256)
        b_n = jnp.concatenate([gathered(b32, 4 * n + m)[...] for m in range(4)]).astype(BF)
        b[here] = b_n
        pre = mm(b_n, w_up[...]) + bias[...]
        cdf = 0.5 * (1.0 + lax.erf(pre * (0.5**0.5)))
        act[here] = (pre * cdf).astype(BF)
        slope = cdf + pre * (jnp.exp(-0.5 * pre * pre) * 0.3989422804014327)
        gpre_n = (mmt(gm[here], w_down[...]) * slope).astype(BF)
        gpre[here] = gpre_n
        back = mmt(gpre_n, w_up[...])
        for m in range(4):
            put_partial(gb, 4 * n + m, back[m * 64 : m * 64 + 64])
        count += rows(gpre_n.astype(F32))
    total[...] = count


def mlp(pieces, *args):
    out = local_call(
        mlp_kernel,
        "mlp",
        8,
        PARTIAL_PIECES
        + (
            shape((1024, 1024), BF),
            shape((1024, 256), BF),
            shape((1024, 256), BF),
            shape((1, 256)),
        ),
        *pieces,
        *args,
    )
    return out[:12], *out[12:]


def by_z(starts, n, high=64):
    return pl.multiple_of(lax.rem(starts[n], 512) // 128 * (2 * high) + (n % 2) * high, 8)


def mlp_down_kernel(starts, act, w, g, bias, mine, other, scale_sum):
    total = bias[...] * rows(g[pl.ds(pl.multiple_of(starts[0], 64), 64)].astype(F32))
    for n in range(4):
        y = mm(act[pl.ds(n * 256, 256)], w[...])
        half = mine if n < 2 else other
        for m in range(4):
            y_m = y[m * 64 : m * 64 + 64]
            half[pl.ds(by_z(starts, 4 * n + m), 64)] = y_m
            at = pl.multiple_of(starts[4 * n + m], 64)
            total += rows(y_m * g[pl.ds(at, 64)].astype(F32))
    scale_sum[...] = total


def mlp_down(*args):
    half = shape((512, 1024))
    return local_call(mlp_down_kernel, "mlp_down", 3, (half, half, shape((1, 1024))), *args)


def grad_middle_kernel(
    gb, hat, std, gain, g, attn, scale, w, gh, ga32, blocks, sums
):
    gb_v, hat_v = gb[...], hat[...]
    gh_v = g[...] + norm_back(gb_v, hat_v, std[...], gain[...])
    gh[...] = gh_v
    ga_v = gh_v * scale[...]
    ga32[...] = ga_v
    ga = ga_v.astype(BF)
    y = mmt(ga, w[...])
    for n in range(8):
        blocks[n] = y[:, n * 128 : n * 128 + 128]
    sums[0:1] = rows(ga.astype(F32))
    sums[1:2] = rows(gb_v * hat_v)
    sums[2:3] = rows(gb_v)
    sums[3:4] = rows(gh_v * attn[...])


def grad_middle(*args):
    wide = shape((64, 1024))
    return local_call(
        grad_middle_kernel,
        "grad_middle",
        1.5,
        (wide, wide, shape((8, 64, 128)), shape((4, 1024))),
        *args,
    )


def attn_backward_kernel(starts, q, k, v, lse, mine, other, mixed, gq_t, g):
    for n in range(16):
        at = pl.ds(pl.multiple_of(lax.rem(starts[n], 512), 64), 64)
        block = mine[at, :64] if n < 8 else other[at]
        g[n * 64 : n * 64 + 64] = block.astype(BF)
    k_t = k[...].astype(F32).T.astype(BF)
    gk = jnp.zeros((1024, 64), F32)
    gv = jnp.zeros((1024, 64), F32)
    for n in range(4):
        here = pl.ds(n * 256, 256)
        gctx_n = g[here]
        q_n = q[here]
        p = jnp.exp(mmt(k[...], q_n) * FACTOR - lse[:, here])
        gv += mm(p.astype(BF), gctx_n)
        gp = mmt(v[...], gctx_n)
        gs = (p * (gp - jnp.sum(p * gp, axis=0, keepdims=True))).astype(BF)
        gk += mm(gs, q_n)
        gq_t[:, here] = mm(k_t, gs)
    mixed[...] = jnp.concatenate([gq_t[...].T * FACTOR, gk * FACTOR, gv], axis=1).astype(BF)


def attn_backward(*args):
    return local_call(
        attn_backward_kernel,
        "attn_backward",
        6,
        shape((1024, 192), BF),
        *args,
        scratch=[pltpu.VMEM((64, 1024), F32), pltpu.VMEM((1024, 64), BF)],
    )


def input_grad_kernel(starts, x, mixed, w, *refs):
    out, (sums, cols) = refs[:12], refs[12:]
    gain_sum = jnp.zeros((1, 1024), F32)
    shift_sum = jnp.zeros((1, 1024), F32)
    for n in (4, 5, 6, 7, 0, 1, 2, 3):
        lo, hi = starts[2 * n], starts[2 * n + 1]
        x_n = jnp.concatenate(
            [x[pl.ds(pl.multiple_of(lo, 64), 64)], x[pl.ds(pl.multiple_of(hi, 64), 64)]]
        ).astype(F32)
        x_hat, _ = normalize(x_n)
        y = mmt(mixed[pl.ds(n * 128, 128)], w[...])
        put_partial(out, 2 * n, y[:64])
        put_partial(out, 2 * n + 1, y[64:])
        gain_sum += rows(y * x_hat)
        shift_sum += rows(y)
    sums[0:1] = gain_sum
    sums[1:2] = shift_sum
    cols[...] = rows(mixed[...].astype(F32))


def input_grad(*args):
    out = local_call(
        input_grad_kernel,
        "input_grad",
        6,
        PARTIAL_PIECES + (shape((2, 1024)), shape((1, 192))),
        *args,
    )
    return out[:12], *out[12:]


def out_grad_kernel(starts, ctx_t, mine, other, out, ga):
    for n in range(16):
        half = mine if n < 8 else other
        ga[n * 64 : n * 64 + 64] = half[pl.ds(by_z(starts, n), 64)].astype(BF)
    y = mm(ctx_t[...], ga[...])
    for n in range(8):
        x, yl = n % 4, n // 4
        out[x * 64 : x * 64 + 64, yl * 128 : yl * 128 + 128] = y[:, n * 128 : n * 128 + 128]


def out_grad(*args):
    return local_call(
        out_grad_kernel,
        "out_grad",
        3,
        shape((256, 256)),
        *args,
        scratch=[pltpu.VMEM((1024, 1024), BF)],
    )


def last_rows_kernel(g, x, gain, gh, out):
    hat, std = normalize(x[...])
    out[...] = gh[...] + norm_back(g[...], hat, std, gain[...])


def last_rows(*args):
    return local_call(last_rows_kernel, "last_rows", 0.5, shape((64, 1024)), *args)


def place_kernel(starts, *refs):
    pieces, out, sems = refs[:10], refs[10], refs[11]
    copies = []
    for n in range(16):
        at = pl.multiple_of(starts[n], 64)
        copies.append(
            pltpu.make_async_copy(gathered(pieces, n), out.at[pl.ds(at, 64)], sems.at[n])
        )
    for copy in copies:
        copy.start()
    for copy in copies:
        copy.wait()


def place(starts, pieces):
    return pl.pallas_call(
        place_kernel,
        out_shape=shape((1024, 1024)),
        in_specs=[SCALARS] + [ON_CHIP] * 10,
        out_specs=pl.BlockSpec(memory_space=pl.ANY),
        scratch_shapes=[pltpu.SemaphoreType.DMA((16,))],
        compiler_params=params(),
        cost_estimate=cost(3),
        name="place",
    )(starts, *pieces)


def place_final_kernel(starts, mine, other, out, sums, sems):
    copies = []
    for n in range(16):
        half = mine if n < 8 else other
        copies.append(
            pltpu.make_async_copy(
                half.at[pl.ds(by_z(starts, n, 72), 64)],
                out.at[pl.ds(pl.multiple_of(starts[n], 64), 64)],
                sems.at[n],
            )
        )
    for copy in copies:
        copy.start()
    total = None
    for half in (mine, other):
        v = [half[n * 144 + 64 : n * 144 + 72] + half[n * 144 + 136 : n * 144 + 144] for n in range(4)]
        v = (v[0] + v[1]) + (v[2] + v[3])
        total = v if total is None else total + v
    sums[...] = total
    for copy in copies:
        copy.wait()


def place_final(starts, mine, other):
    return pl.pallas_call(
        place_final_kernel,
        out_shape=(shape((1024, 1024)), shape((8, 1024))),
        in_specs=[SCALARS, ON_CHIP, ON_CHIP],
        out_specs=(pl.BlockSpec(memory_space=pl.ANY), ON_CHIP),
        scratch_shapes=[pltpu.SemaphoreType.DMA((16,))],
        compiler_params=params(),
        cost_estimate=cost(3),
        name="place_final",
    )(starts, mine, other)


def on_device(
    images,
    w_qkv,
    bias_query,
    bias_value,
    w_out,
    bias_out,
    w_up,
    bias_up,
    w_down,
    bias_down,
    norm1_gain,
    norm1_shift,
    norm2_gain,
    norm2_shift,
    scale_attn,
    scale_mlp,
    cotangent,
):
    w_qkv, w_out, w_up, w_down = w_qkv[0], w_out[0], w_up[0], w_down[0]
    images, cotangent = images[0], cotangent[0]
    c, z, yh = lax.axis_index("c"), lax.axis_index("z"), lax.axis_index("yh")
    starts = jnp.stack(
        [
            (((c + i) % 2) * 8 + ((z + k) % 4) * 2 + ((yh + j) % 2)) * 64
            for i in range(2)
            for k in range(4)
            for j in range(2)
        ]
    )
    x_own = lax.dynamic_slice_in_dim(images, starts[0], 64, 0).astype(F32)
    g_own = lax.dynamic_slice_in_dim(cotangent, starts[0], 64, 0).astype(F32)

    w_near = hold(gather_near(w_out.astype(F32)))
    w_half = gather_far(*w_near)
    a, q, k, v, lse, ctx_mine, ctx_other, ctx_t = attn_forward(
        starts,
        hold(images, w_near),
        w_qkv,
        bias_query,
        bias_value,
        norm1_gain,
        norm1_shift,
    )
    pair = jnp.concatenate([ctx_mine, from_core(ctx_other)], axis=1)
    ctx_own = swap_chips(pair.reshape(8, 64, 128))
    w_full = round_weights(starts, gather_core(hold(w_half, pair)))
    attn, hmid, b_hat, b_std, b_own = middle(
        ctx_own, w_full, x_own, bias_out, scale_attn, norm2_gain, norm2_shift
    )
    b_near = gather_near(b_own)
    gm = grad_rows(starts, hold(cotangent, b_own), scale_mlp)
    b_half = gather_far(*hold(b_near))
    gb_part, b, act, gpre, sum_gpre = mlp(gather_core(b_half), gm, w_up, w_down, bias_up)

    gb_u = hold(scatter_add(gb_part, scatter_core(gb_part)))
    gb_near = hold(scatter_near(gb_u))
    act, gpre = hold((act, gpre), gb_u)
    mlp_mine, mlp_other, scale_sum = mlp_down(starts, act, w_down, cotangent, bias_down)
    gb_q = hold(scatter_join(gb_u, gb_near))
    mlp_u = mlp_mine + hold(from_core(mlp_other), gb_q)
    left, right = slice(0, 512), slice(512, 1024)
    b, gm_late = hold((b, gm), gb_q)
    ff = [
        tmm(b[:, left], gpre),
        tmm(gm_late[:, left], act),
        tmm(b[:, right], gpre),
        tmm(gm_late[:, right], act),
    ]
    gb_far, ff = hold((scatter_far(gb_q), ff), mlp_u)
    gb = scatter_end(gb_u, gb_near, gb_far)
    mlp_z = lax.psum_scatter(mlp_u, "z", scatter_dimension=0, tiled=True)
    gh, ga32, gctx_blocks, mid_sums = grad_middle(
        gb, b_hat, b_std, norm2_gain, g_own, attn, scale_attn, w_full
    )
    ga_other = from_yh(ga32)
    gctx = swap_chips(gctx_blocks).reshape(512, 128)
    gctx_other = from_core(gctx[:, 64:])
    ga_other, gctx, mlp_z = hold((ga_other, gctx, mlp_z))
    ga_half = lax.all_gather(jnp.concatenate([ga32, ga_other]), "z", axis=0, tiled=True)
    ff_x = sum_images(*ff)
    mlp_far = from_yh(mlp_z[64:])
    g_mixed = attn_backward(starts, q, k, v, lse, gctx, gctx_other)

    ga_part, norm1_sums, sum_mixed = input_grad(starts, images, g_mixed, w_qkv)
    in_u, mlp_far = hold((scatter_add(ga_part, scatter_core(ga_part)), mlp_far))
    in_near = scatter_near(in_u)
    final = jnp.concatenate(
        [
            hmid + scale_mlp * (mlp_z[:64] + mlp_far + bias_down),
            mid_sums,
            rows(gm[:64].astype(F32)),
            norm1_sums,
            scale_sum,
        ]
    )
    final_near = from_yh(final)

    in_near, final_near, ga_half = hold((in_near, final_near, ga_half))
    in_far = scatter_far(scatter_join(in_u, in_near))
    final_half = lax.all_gather(
        jnp.concatenate([final, final_near]), "z", axis=0, tiled=True
    )
    grad_out = out_grad(starts, ctx_t, ga_half, from_core(ga_half))
    in_far, grad_out = hold((in_far, grad_out))
    g_norm1 = scatter_end(in_u, in_near, in_far)
    grad_in = last_rows(g_norm1, x_own, norm1_gain, gh)

    end_near = gather_near(grad_in)
    a_late = hold(a, in_u)
    qkv_x = sum_images(tmm(a_late[:, left], g_mixed), tmm(a_late[:, right], g_mixed))
    out_x = sum_images(grad_out)
    end_near, final_half, ff_x = hold((end_near, final_half, ff_x))
    end_half = gather_far(*end_near)
    final_all, wide = place_final(starts, final_half, from_core(final_half))
    narrow = jnp.concatenate(
        [sum_mixed[:, :64], sum_mixed[:, 128:], sum_gpre, jnp.zeros((1, 640), F32)], axis=1
    )
    sums = jnp.concatenate([wide, jnp.broadcast_to(narrow, (8, 1024))])
    upper = lax.axis_index("yl") == 1
    ff_x, qkv_x, out_x = hold((ff_x, qkv_x, out_x), end_half[3])

    def kept(side):
        return jnp.concatenate([halves(ff_x, side), halves(qkv_x, side)], axis=1)

    weight_grads = kept(upper) + lax.ppermute(kept(~upper), "yl", [(0, 1), (1, 0)])
    grad_out = halves(out_x, upper) + lax.ppermute(
        halves(out_x, ~upper), "yl", [(0, 1), (1, 0)]
    )
    sums = pair_sum(sums, "yl")
    end_half, sums, weight_grads, grad_out = hold((end_half, sums, weight_grads, grad_out))
    sums = ring_sum(sums, "x")
    grad_input = place(starts, gather_core(end_half))

    return (
        final_all[None],
        grad_input[None],
        weight_grads[None, :, 512:],
        sums[8:9, :64],
        sums[8:9, 64:128],
        grad_out[None],
        sums[0:1],
        weight_grads[None, :, :256],
        sums[8:9, 128:384],
        weight_grads[:, 256:512].T[None],
        sums[4:5],
        sums[5:6],
        sums[6:7],
        sums[1:2],
        sums[2:3],
        sums[3:4],
        sums[7:8],
    )


def solution(mesh):
    fine = Mesh(mesh.devices.reshape(2, 4, 4, 2, 2), ("yl", "x", "z", "yh", "c"))
    return jax.shard_map(
        on_device,
        mesh=fine,
        in_specs=(
            P(DATA, None, None),
            P(None, None, TENSOR),
            P(None, TENSOR),
            P(None, TENSOR),
            P(None, TENSOR, None),
            P(),
            P(None, None, TENSOR),
            P(None, TENSOR),
            P(None, TENSOR, None),
            P(),
            P(),
            P(),
            P(),
            P(),
            P(),
            P(),
            P(DATA, None, None),
        ),
        out_specs=(
            P(DATA, None, None),
            P(DATA, None, None),
            P(None, DATA, TENSOR),
            P(None, TENSOR),
            P(None, TENSOR),
            P(None, TENSOR, DATA),
            P(),
            P(None, DATA, TENSOR),
            P(None, TENSOR),
            P(None, TENSOR, DATA),
            P(),
            P(),
            P(),
            P(),
            P(),
            P(),
            P(),
        ),
        check_vma=False,
    )
```
